32 devices in a mesh: fsdp: 8 (over y, x, core), rep: 4 (over z).
Axes of the slice: x: 2, y: 2, z: 4, core: 2. Of those that a mesh axis runs over, the one named last changes fastest.
Arguments:
- grads: bfloat16 [8, 1024, 1024], P('rep', 'fsdp'), may hold values from -6 to 6
- second_moment: bfloat16 [8, 1024, 1024], P('rep', 'fsdp'), may hold values from 0.0099487305 to 1
- root_factors: bfloat16 [4, 8, 1024, 1024], P('rep', 'fsdp')
- block_shape: int32 [8, 2], replicated, may hold values from 128 to 1024, as said below
- block_owner: int32 [8], replicated, may hold values from 0 to 7, as said below
Outputs:
- direction: bfloat16 [8, 1024, 1024], P('rep', 'fsdp')
The draws below stay inside these ranges and needn't reach their ends.
Inputs may be any that keep to these rules, and one draw needn't show every extreme that they name: `block_owner`: the 4 blocks of rep indices 2k and 2k+1 have distinct owners. `block_shape`: each entry is 1024 or a tail of at least 128.
All inputs are finite; a program needn't handle non-finite values.
Results may differ from the reference program's by a relative error of at most 0.0057.
Values may be sent and summed in bfloat16 or wider, within the bound.
A program may use at most 64 MiB of HBM per device.

```python
import math
import jax
import jax.numpy as jnp
from jax import lax

BS = 1024
BLK_REP = 2
NB = 8
N_FSDP = 8
N_REP = 4


def draw_root_factors(key, part):
    key = jax.random.fold_in(key, 7)
    noise = jax.random.normal(key, (N_REP, N_FSDP, BS, BS), jnp.float32)
    sym = (noise + jnp.swapaxes(noise, 2, 3)) * (0.70710678 / math.sqrt(BS))
    return (3.0 * jnp.eye(BS, dtype=jnp.float32) + sym).astype(jnp.bfloat16)


def draw_block_shape(key, part):
    key = jax.random.fold_in(key, 11)
    first, second = jax.random.split(key)
    ragged = jax.random.randint(first, (NB, 2), 0, 4) == 0
    tails = jax.random.randint(second, (NB, 2), BS // 8, BS)
    shapes = jnp.where(ragged, tails, BS).astype(jnp.int32)
    shapes = shapes.at[0].set(BS)
    return shapes.at[NB - 1, 1].set(BS // 8)


def draw_block_owner(key, part):
    key = jax.random.fold_in(key, 13)
    keys = jax.random.split(key, N_REP // 2)

    def one_pair(pair_key):
        first, second = jax.random.split(pair_key)
        middle = jax.random.permutation(first, N_FSDP - 2)[:2 * BLK_REP - 2] + 1
        chosen = jnp.concatenate([jnp.array([0, N_FSDP - 1], jnp.int32), middle.astype(jnp.int32)])
        return chosen[jax.random.permutation(second, 2 * BLK_REP)]
    return jax.vmap(one_pair)(keys).reshape(-1).astype(jnp.int32)


def steps_of(key, extent, shards, smallest, top_value):
    gain, own = 1.0, jax.random.fold_in(key, 6)
    for position, blocks in shards:
        heights = jnp.exp(jax.random.uniform(jax.random.fold_in(own, position), (blocks,), jnp.float32, smallest / len(shards), top_value / len(shards)))
        gain = gain * jnp.repeat(heights, extent[position] // blocks).reshape([-1 if axis == position else 1 for axis in range(len(extent))])
    return gain


def centred(rng, dims, scale, bound, shards=(), kind=jnp.bfloat16):
    loudness = steps_of(rng, dims, shards, -0.22, 0.18) if shards else 1.0
    values = jax.random.normal(rng, dims, jnp.float32) * scale * loudness
    return jnp.minimum(jnp.maximum(values, -bound), bound).astype(kind)


def setup_inputs(seed: int = 0) -> dict:
    seeds = jax.random.split(jax.random.key(seed), 6)
    grads = centred(seeds[0], (NB, BS, BS), 1.0, 6.0, ((0, 4), (1, 8)))
    second_moment = jnp.clip(jnp.exp(math.log(1.0) - 4.61031033 * jax.random.uniform(seeds[1], (NB, BS, BS), jnp.float32) ** steps_of(seeds[1], (NB, BS, BS), ((0, 4), (1, 8)), -0.2, 0.2)), 0.0099487305, 1.0).astype(jnp.bfloat16)
    root_factors = draw_root_factors(jax.random.fold_in(seeds[5], 71), 0)
    block_shape = draw_block_shape(jax.random.fold_in(seeds[5], 71), 0)
    block_owner = draw_block_owner(jax.random.fold_in(seeds[5], 71), 0)
    return {"grads": grads, "second_moment": second_moment, "root_factors": root_factors, "block_shape": block_shape, "block_owner": block_owner}


ADAM_EPS = 1e-08
NORM_EPS = 1e-06

def reference(grads, second_moment, root_factors, block_shape, block_owner):
    total = grads.shape[0]
    width = grads.shape[1]
    line = jnp.arange(width, dtype=jnp.int32)

    def one_block(index):
        shape = block_shape[index]
        inside = (line[:, None] < shape[0]) & (line[None, :] < shape[1])
        masked = jnp.where(inside, grads[index], jnp.zeros((width, width), grads.dtype))
        adam = masked.astype(jnp.float32) / (jnp.sqrt(second_moment[index].astype(jnp.float32)) + ADAM_EPS)
        adam_sq = jnp.sum(adam * adam)
        pair = (index // (2 * BLK_REP)).astype(jnp.int32)
        owner = block_owner[index]
        right = root_factors[2 * pair, owner]
        left = root_factors[2 * pair + 1, owner]
        half = jnp.dot(masked, right, preferred_element_type=jnp.float32).astype(jnp.bfloat16)
        full = jnp.dot(left, half, preferred_element_type=jnp.float32)
        shampoo = jnp.where(inside, full, jnp.zeros_like(full)).astype(jnp.bfloat16)
        wide = shampoo.astype(jnp.float32)
        shampoo_sq = jnp.sum(wide * wide)
        ratio = jnp.sqrt(adam_sq) / jnp.sqrt(shampoo_sq + NORM_EPS)
        return (wide * ratio).astype(jnp.bfloat16)
    return lax.map(one_block, jnp.arange(total, dtype=jnp.int32))
```

```python
import functools

import jax
import jax.numpy as jnp
from jax import lax
from jax.experimental import pallas as pl
from jax.experimental.pallas import tpu as pltpu
from jax.sharding import PartitionSpec as P

ADAM_EPS = 1e-08
NORM_EPS = 1e-06
MESH = pl.DeviceIdType.MESH


def flipped(index, mask, extent):
    out, bit = 0, 1
    while bit < extent:
        out = out + bit * (((index // bit) % 2 + (mask // bit) % 2) % 2)
        bit *= 2
    return out


def fold(square):
    rows, columns = square.shape
    tall = jnp.sum(square.reshape(rows // 8, 8, columns), axis=0)
    return functools.reduce(
        lambda a, b: a + b, [tall[:, i : i + 128] for i in range(0, columns, 128)]
    )


def kernel(
    n, step_rows, col_chunks,
    shape_ref, owner_ref, grads_ref, moment_ref, factor_ref, out_ref,
    outbound, g_full, own, other_rows, other_cols, half, s_rows, s_cols,
    r_rows, r_cols, adam_out, adam_in, sq_out, sq_in,
    own_sem, g_send, g_recv, a_send, a_recv, q_send, q_recv,
    zr_send, zr_recv, zc_send, zc_recv, sr_send, sr_recv, sc_send, sc_recv,
):
    count, band, width = grads_ref.shape
    me = lax.axis_index("fsdp")
    rep = lax.axis_index("rep")
    parity = rep % 2
    partner = rep + 1 - 2 * parity
    col_width = width // col_chunks
    row_chunks = width // step_rows
    group = step_rows // band
    first = rep * count

    barrier = pltpu.get_barrier_semaphore()

    @pl.loop(1, n)
    def _(t):
        pl.semaphore_signal(
            barrier, inc=1, device_id=(flipped(me, t, n), rep), device_id_type=MESH
        )

    pl.semaphore_signal(barrier, inc=1, device_id=(me, partner), device_id_type=MESH)

    own_copy = pltpu.make_async_copy(factor_ref.at[0, 0], own, own_sem)
    own_copy.start()

    def rows_of(index):
        return pl.ds(pl.multiple_of(index * band, band), band)

    line = me * band + lax.broadcasted_iota(jnp.int32, (band, width), 0)
    column = lax.broadcasted_iota(jnp.int32, (band, width), 1)
    masked = []
    for b in range(count):
        inside = (line < shape_ref[first + b, 0]) & (column < shape_ref[first + b, 1])
        wide = jnp.where(inside, grads_ref[b].astype(jnp.float32), 0.0)
        out_ref[b] = wide.astype(jnp.bfloat16)

    def fill(d):
        slot = jnp.zeros((band, width), jnp.bfloat16)
        for b in range(count):
            slot = jnp.where(owner_ref[first + b] == d, out_ref[b], slot)
        return slot

    @pl.loop(0, n)
    def _(d):
        outbound[d] = fill(d)

    g_full[rows_of(me)] = outbound[me]

    pl.semaphore_wait(barrier, n)

    def z_rows(s):
        chunk = flipped(me // group, row_chunks - 1 - s, row_chunks)
        rows = pl.ds(pl.multiple_of(chunk * step_rows, step_rows), step_rows)
        return pltpu.make_async_remote_copy(
            src_ref=factor_ref.at[0, 0, rows], dst_ref=other_rows.at[rows],
            send_sem=zr_send.at[s], recv_sem=zr_recv.at[s],
            device_id=(me, partner), device_id_type=MESH,
        )

    def z_cols(c):
        columns = pl.ds(c * col_width, col_width)
        return pltpu.make_async_remote_copy(
            src_ref=factor_ref.at[0, 0, :, columns], dst_ref=other_cols.at[c],
            send_sem=zc_send.at[c], recv_sem=zc_recv.at[c],
            device_id=(me, partner), device_id_type=MESH,
        )

    @pl.when(parity == 1)
    def _():
        for s in range(row_chunks):
            z_rows(s).start()

    @pl.when(parity == 0)
    def _():
        for c in range(col_chunks):
            z_cols(c).start()

    def peer_copy(source, target, send, recv, peer):
        return pltpu.make_async_remote_copy(
            src_ref=source, dst_ref=target, send_sem=send, recv_sem=recv,
            device_id=(peer, rep), device_id_type=MESH,
        )

    def g_copy(t, landing):
        peer = flipped(me, t, n)
        return peer_copy(
            outbound.at[peer], g_full.at[rows_of(landing)], g_send.at[t], g_recv.at[t], peer
        )

    @pl.loop(1, n)
    def _(s):
        g_copy(n - s, me).start()

    for b in range(count):
        adam = out_ref[b].astype(jnp.float32) / (
            jnp.sqrt(moment_ref[b].astype(jnp.float32)) + ADAM_EPS
        )
        adam_out[b] = fold(adam * adam)
    adam_in[me] = adam_out[...]

    def a_copy(t, landing):
        peer = flipped(me, t, n)
        return peer_copy(adam_out, adam_in.at[landing], a_send.at[t], a_recv.at[t], peer)

    def q_copy(t, landing):
        peer = flipped(me, t, n)
        return peer_copy(sq_out, sq_in.at[landing], q_send.at[t], q_recv.at[t], peer)

    @pl.loop(1, n)
    def _(t):
        a_copy(t, me).start()

    team_rows = jnp.int32(0)
    team_cols = jnp.int32(0)
    for b in range(count):
        mine = owner_ref[first + b] == me
        team_rows += jnp.where(mine, shape_ref[first + b, 0], 0)
        team_cols += jnp.where(mine, shape_ref[first + b, 1], 0)

    def clipped(full, row0, col0):
        r = row0 + lax.broadcasted_iota(jnp.int32, full.shape, 0)
        c = col0 + lax.broadcasted_iota(jnp.int32, full.shape, 1)
        return jnp.where((r < team_rows) & (c < team_cols), full, 0.0).astype(jnp.bfloat16)

    own_copy.wait()

    def sr_copy(t, landing):
        peer = flipped(me, t, n)
        return peer_copy(
            s_rows.at[rows_of(peer)], r_rows.at[landing], sr_send.at[t], sr_recv.at[t], peer
        )

    def sc_copy(t, c, landing):
        peer = flipped(me, t, n)
        return peer_copy(
            s_cols.at[c, rows_of(peer)], r_cols.at[landing, c],
            sc_send.at[t, c], sc_recv.at[t, c], peer,
        )

    @pl.when(parity == 0)
    def _():
        @pl.loop(0, n)
        def _(t):
            source = flipped(me, t, n)

            @pl.when(t != 0)
            def _():
                g_copy(t, source).wait_recv()

            half[rows_of(source)] = jnp.dot(
                g_full[rows_of(source)], own[...], preferred_element_type=jnp.float32
            ).astype(jnp.bfloat16)

        sq_out[...] = jnp.zeros_like(sq_out)

        @pl.loop(0, row_chunks)
        def _(s):
            z_rows(s).wait_recv()
            chunk = flipped(me // group, row_chunks - 1 - s, row_chunks)
            row0 = pl.multiple_of(chunk * step_rows, step_rows)
            full = jnp.dot(
                other_rows[pl.ds(row0, step_rows)], half[...],
                preferred_element_type=jnp.float32,
            )
            part = clipped(full, row0, 0)
            s_rows[pl.ds(row0, step_rows)] = part
            for i in range(group):
                t = (row_chunks - 1 - s) * group + i

                @pl.when(t != 0)
                def _():
                    sr_copy(t, me).start()

            wide = part.astype(jnp.float32)
            sq_out[...] += fold(wide * wide)

        r_rows[me] = s_rows[rows_of(me)]

    @pl.when(parity == 1)
    def _():
        @pl.loop(1, n)
        def _(t):
            g_copy(t, flipped(me, t, n)).wait_recv()

        sq_out[...] = jnp.zeros_like(sq_out)

        @pl.loop(0, col_chunks)
        def _(c):
            pltpu.make_async_remote_copy(
                src_ref=other_cols.at[c], dst_ref=other_cols.at[c],
                send_sem=zc_send.at[c], recv_sem=zc_recv.at[c],
                device_id=(me, partner), device_id_type=MESH,
            ).wait_recv()
            h = jnp.dot(
                g_full[...], other_cols[c], preferred_element_type=jnp.float32
            ).astype(jnp.bfloat16)
            full = jnp.dot(own[...], h, preferred_element_type=jnp.float32)
            part = clipped(full, 0, c * col_width)
            s_cols[c] = part

            @pl.loop(1, n)
            def _(s):
                sc_copy(n - s, c, me).start()

            wide = part.astype(jnp.float32)
            sq_out[...] += fold(wide * wide)
            r_cols[me, c] = s_cols[c, rows_of(me)]

    @pl.loop(1, n)
    def _(t):
        q_copy(t, me).start()

    sq_in[me] = sq_out[...]

    @pl.loop(1, n)
    def _(t):
        a_copy(t, flipped(me, t, n)).wait_recv()

    adam_sum = jnp.sum(adam_in[...], axis=0)

    @pl.loop(1, n)
    def _(t):
        q_copy(t, flipped(me, t, n)).wait_recv()

    ratios = []
    for b in range(count):
        adam_sq = jnp.sum(adam_sum[b], keepdims=True)
        shampoo_sq = jnp.sum(sq_in[owner_ref[first + b]], keepdims=True)
        ratios.append(jnp.sqrt(adam_sq) / jnp.sqrt(shampoo_sq + NORM_EPS))

    @pl.when(parity == 0)
    def _():
        @pl.loop(1, n)
        def _(t):
            sr_copy(t, flipped(me, t, n)).wait_recv()

        for b in range(count):
            wide = r_rows[owner_ref[first + b]].astype(jnp.float32)
            out_ref[b] = (wide * ratios[b]).astype(jnp.bfloat16)

        @pl.loop(1, n)
        def _(t):
            sr_copy(t, me).wait_send()

        for c in range(col_chunks):
            z_cols(c).wait_send()

    @pl.when(parity == 1)
    def _():
        @pl.loop(1, n)
        def _(t):
            for c in range(col_chunks):
                sc_copy(t, c, flipped(me, t, n)).wait_recv()

        for b in range(count):
            for c in range(col_chunks):
                wide = r_cols[owner_ref[first + b], c].astype(jnp.float32)
                out_ref[b, :, c * col_width : (c + 1) * col_width] = (
                    wide * ratios[b]
                ).astype(jnp.bfloat16)

        @pl.loop(1, n)
        def _(t):
            for c in range(col_chunks):
                sc_copy(t, c, me).wait_send()

        for s in range(row_chunks):
            z_rows(s).wait_send()

    @pl.loop(1, n)
    def _(t):
        g_copy(t, me).wait_send()
        a_copy(t, me).wait_send()
        q_copy(t, me).wait_send()


def on_device(grads, second_moment, root_factors, block_shape, block_owner):
    count, band, width = grads.shape
    n = lax.axis_size("fsdp")
    step_rows = max(band, 128)
    col_chunks = 8 if n <= 8 else 2
    row_chunks = width // step_rows
    col_width = width // col_chunks
    vmem = pl.BlockSpec(memory_space=pltpu.VMEM)
    smem = pl.BlockSpec(memory_space=pltpu.SMEM)
    bf16, f32 = jnp.bfloat16, jnp.float32
    dma = pltpu.SemaphoreType.DMA
    return pl.pallas_call(
        functools.partial(kernel, n, step_rows, col_chunks),
        out_shape=jax.ShapeDtypeStruct(grads.shape, bf16),
        in_specs=[smem, smem, vmem, vmem, pl.BlockSpec(memory_space=pl.ANY)],
        out_specs=vmem,
        scratch_shapes=[
            pltpu.VMEM((n, band, width), bf16),
            pltpu.VMEM((width, width), bf16),
            pltpu.VMEM((width, width), bf16),
            pltpu.VMEM((width, width), bf16),
            pltpu.VMEM((col_chunks, width, col_width), bf16),
            pltpu.VMEM((width, width), bf16),
            pltpu.VMEM((width, width), bf16),
            pltpu.VMEM((col_chunks, width, col_width), bf16),
            pltpu.VMEM((n, band, width), bf16),
            pltpu.VMEM((n, col_chunks, band, col_width), bf16),
            pltpu.VMEM((count, 8, 128), f32),
            pltpu.VMEM((n, count, 8, 128), f32),
            pltpu.VMEM((8, 128), f32),
            pltpu.VMEM((n, 8, 128), f32),
            dma,
            dma((n,)), dma((n,)), dma((n,)), dma((n,)), dma((n,)), dma((n,)),
            dma((row_chunks,)), dma((row_chunks,)),
            dma((col_chunks,)), dma((col_chunks,)),
            dma((n,)), dma((n,)),
            dma((n, col_chunks)), dma((n, col_chunks)),
        ],
        compiler_params=pltpu.CompilerParams(
            collective_id=0, has_side_effects=True, vmem_limit_bytes=44 * 1024 * 1024
        ),
        cost_estimate=pl.CostEstimate(
            flops=4 * width**3, bytes_accessed=4 * 1024 * 1024, transcendentals=0
        ),
    )(block_shape, block_owner, grads, second_moment, root_factors)


def solution(mesh):
    placed = (
        P("rep", "fsdp", None),
        P("rep", "fsdp", None),
        P("rep", "fsdp", None, None),
        P(),
        P(),
    )
    return jax.shard_map(
        on_device, mesh=mesh, in_specs=placed, out_specs=P("rep", "fsdp", None), check_vma=False
    )
```

```python
import functools

import jax
import jax.numpy as jnp
from jax import lax
from jax.experimental import pallas as pl
from jax.experimental.pallas import tpu as pltpu
from jax.sharding import PartitionSpec as P

ADAM_EPS = 1e-08
NORM_EPS = 1e-06
MESH = pl.DeviceIdType.MESH


def flipped(index, mask, extent):
    out, bit = 0, 1
    while bit < extent:
        out = out + bit * (((index // bit) % 2 + (mask // bit) % 2) % 2)
        bit *= 2
    return out


def fold(square):
    rows, columns = square.shape
    tall = jnp.sum(square.reshape(rows // 8, 8, columns), axis=0)
    return functools.reduce(
        lambda a, b: a + b, [tall[:, i : i + 128] for i in range(0, columns, 128)]
    )


def kernel(
    n, step_rows, col_chunks,
    shape_hbm, owner_hbm, grads_hbm, moment_hbm, factor_ref, out_ref,
    shape_ref, owner_ref, grads_ref, moment_ref, load_sem,
    outbound, g_full, own, other_rows, other_cols, half, s_rows, s_cols,
    r_rows, r_cols, adam_out, adam_in, sq_out, sq_in,
    own_sem, g_send, g_recv, a_send, a_recv, q_send, q_recv,
    zr_send, zr_recv, zc_send, zc_recv, sr_send, sr_recv, sc_send, sc_recv,
):
    count, band, width = grads_ref.shape
    me = lax.axis_index("fsdp")
    rep = lax.axis_index("rep")
    parity = rep % 2
    partner = rep + 1 - 2 * parity
    col_width = width // col_chunks
    row_chunks = width // step_rows
    group = step_rows // band
    first = rep * count

    barrier = pltpu.get_barrier_semaphore()

    @pl.loop(1, n)
    def _(t):
        pl.semaphore_signal(
            barrier, inc=1, device_id=(flipped(me, t, n), rep), device_id_type=MESH
        )

    pl.semaphore_signal(barrier, inc=1, device_id=(me, partner), device_id_type=MESH)

    loads = [
        pltpu.make_async_copy(source, target, load_sem.at[i])
        for i, (source, target) in enumerate([
            (shape_hbm, shape_ref), (owner_hbm, owner_ref),
            (grads_hbm, grads_ref), (moment_hbm, moment_ref),
        ])
    ]
    for load in loads:
        load.start()
    own_copy = pltpu.make_async_copy(factor_ref.at[0, 0], own, own_sem)
    own_copy.start()

    def rows_of(index):
        return pl.ds(pl.multiple_of(index * band, band), band)

    pl.semaphore_wait(barrier, n)

    def z_rows(s):
        chunk = flipped(me // group, row_chunks - 1 - s, row_chunks)
        rows = pl.ds(pl.multiple_of(chunk * step_rows, step_rows), step_rows)
        return pltpu.make_async_remote_copy(
            src_ref=factor_ref.at[0, 0, rows], dst_ref=other_rows.at[rows],
            send_sem=zr_send.at[s], recv_sem=zr_recv.at[s],
            device_id=(me, partner), device_id_type=MESH,
        )

    def z_cols(c):
        columns = pl.ds(c * col_width, col_width)
        return pltpu.make_async_remote_copy(
            src_ref=factor_ref.at[0, 0, :, columns], dst_ref=other_cols.at[c],
            send_sem=zc_send.at[c], recv_sem=zc_recv.at[c],
            device_id=(me, partner), device_id_type=MESH,
        )

    @pl.when(parity == 1)
    def _():
        for s in range(row_chunks):
            z_rows(s).start()

    @pl.when(parity == 0)
    def _():
        for c in range(col_chunks):
            z_cols(c).start()

    for load in loads[:3]:
        load.wait()

    line = me * band + lax.broadcasted_iota(jnp.int32, (band, width), 0)
    column = lax.broadcasted_iota(jnp.int32, (band, width), 1)
    masked = []
    for b in range(count):
        inside = (line < shape_ref[0, first + b]) & (column < shape_ref[1, first + b])
        wide = jnp.where(inside, grads_ref[b].astype(jnp.float32), 0.0)
        out_ref[b] = wide.astype(jnp.bfloat16)

    def fill(d):
        slot = jnp.zeros((band, width), jnp.bfloat16)
        for b in range(count):
            slot = jnp.where(owner_ref[first + b] == d, out_ref[b], slot)
        return slot

    @pl.loop(0, n)
    def _(d):
        outbound[d] = fill(d)

    g_full[rows_of(me)] = outbound[me]

    def peer_copy(source, target, send, recv, peer):
        return pltpu.make_async_remote_copy(
            src_ref=source, dst_ref=target, send_sem=send, recv_sem=recv,
            device_id=(peer, rep), device_id_type=MESH,
        )

    def g_copy(t, landing):
        peer = flipped(me, t, n)
        return peer_copy(
            outbound.at[peer], g_full.at[rows_of(landing)], g_send.at[t], g_recv.at[t], peer
        )

    @pl.loop(1, n)
    def _(s):
        g_copy(n - s, me).start()

    loads[3].wait()

    for b in range(count):
        adam = out_ref[b].astype(jnp.float32) / (
            jnp.sqrt(moment_ref[b].astype(jnp.float32)) + ADAM_EPS
        )
        adam_out[b] = fold(adam * adam)
    adam_in[me] = adam_out[...]

    def a_copy(t, landing):
        peer = flipped(me, t, n)
        return peer_copy(adam_out, adam_in.at[landing], a_send.at[t], a_recv.at[t], peer)

    def q_copy(t, landing):
        peer = flipped(me, t, n)
        return peer_copy(sq_out, sq_in.at[landing], q_send.at[t], q_recv.at[t], peer)

    @pl.loop(1, n)
    def _(t):
        a_copy(t, me).start()

    team_rows = jnp.int32(0)
    team_cols = jnp.int32(0)
    for b in range(count):
        mine = owner_ref[first + b] == me
        team_rows += jnp.where(mine, shape_ref[0, first + b], 0)
        team_cols += jnp.where(mine, shape_ref[1, first + b], 0)

    def clipped(full, row0, col0):
        r = row0 + lax.broadcasted_iota(jnp.int32, full.shape, 0)
        c = col0 + lax.broadcasted_iota(jnp.int32, full.shape, 1)
        return jnp.where((r < team_rows) & (c < team_cols), full, 0.0).astype(jnp.bfloat16)

    own_copy.wait()

    def sr_copy(t, landing):
        peer = flipped(me, t, n)
        return peer_copy(
            s_rows.at[rows_of(peer)], r_rows.at[landing], sr_send.at[t], sr_recv.at[t], peer
        )

    def sc_copy(t, c, landing):
        peer = flipped(me, t, n)
        return peer_copy(
            s_cols.at[c, rows_of(peer)], r_cols.at[landing, c],
            sc_send.at[t, c], sc_recv.at[t, c], peer,
        )

    @pl.when(parity == 0)
    def _():
        @pl.loop(0, n)
        def _(t):
            source = flipped(me, t, n)

            @pl.when(t != 0)
            def _():
                g_copy(t, source).wait_recv()

            half[rows_of(source)] = jnp.dot(
                g_full[rows_of(source)], own[...], preferred_element_type=jnp.float32
            ).astype(jnp.bfloat16)

        sq_out[...] = jnp.zeros_like(sq_out)

        @pl.loop(0, row_chunks)
        def _(s):
            z_rows(s).wait_recv()
            chunk = flipped(me // group, row_chunks - 1 - s, row_chunks)
            row0 = pl.multiple_of(chunk * step_rows, step_rows)
            full = jnp.dot(
                other_rows[pl.ds(row0, step_rows)], half[...],
                preferred_element_type=jnp.float32,
            )
            part = clipped(full, row0, 0)
            s_rows[pl.ds(row0, step_rows)] = part
            for i in range(group):
                t = (row_chunks - 1 - s) * group + i

                @pl.when(t != 0)
                def _():
                    sr_copy(t, me).start()

            wide = part.astype(jnp.float32)
            sq_out[...] += fold(wide * wide)

        r_rows[me] = s_rows[rows_of(me)]

    @pl.when(parity == 1)
    def _():
        @pl.loop(1, n)
        def _(t):
            g_copy(t, flipped(me, t, n)).wait_recv()

        sq_out[...] = jnp.zeros_like(sq_out)

        @pl.loop(0, col_chunks)
        def _(c):
            pltpu.make_async_remote_copy(
                src_ref=other_cols.at[c], dst_ref=other_cols.at[c],
                send_sem=zc_send.at[c], recv_sem=zc_recv.at[c],
                device_id=(me, partner), device_id_type=MESH,
            ).wait_recv()
            h = jnp.dot(
                g_full[...], other_cols[c], preferred_element_type=jnp.float32
            ).astype(jnp.bfloat16)
            full = jnp.dot(own[...], h, preferred_element_type=jnp.float32)
            part = clipped(full, 0, c * col_width)
            s_cols[c] = part

            @pl.loop(1, n)
            def _(s):
                sc_copy(n - s, c, me).start()

            wide = part.astype(jnp.float32)
            sq_out[...] += fold(wide * wide)
            r_cols[me, c] = s_cols[c, rows_of(me)]

    @pl.loop(1, n)
    def _(t):
        q_copy(t, me).start()

    sq_in[me] = sq_out[...]

    @pl.loop(1, n)
    def _(t):
        a_copy(t, flipped(me, t, n)).wait_recv()

    adam_sum = jnp.sum(adam_in[...], axis=0)

    @pl.loop(1, n)
    def _(t):
        q_copy(t, flipped(me, t, n)).wait_recv()

    ratios = []
    for b in range(count):
        adam_sq = jnp.sum(adam_sum[b], keepdims=True)
        shampoo_sq = jnp.sum(sq_in[owner_ref[first + b]], keepdims=True)
        ratios.append(jnp.sqrt(adam_sq) / jnp.sqrt(shampoo_sq + NORM_EPS))

    @pl.when(parity == 0)
    def _():
        @pl.loop(1, n)
        def _(t):
            sr_copy(t, flipped(me, t, n)).wait_recv()

        for b in range(count):
            wide = r_rows[owner_ref[first + b]].astype(jnp.float32)
            out_ref[b] = (wide * ratios[b]).astype(jnp.bfloat16)

        @pl.loop(1, n)
        def _(t):
            sr_copy(t, me).wait_send()

        for c in range(col_chunks):
            z_cols(c).wait_send()

    @pl.when(parity == 1)
    def _():
        @pl.loop(1, n)
        def _(t):
            for c in range(col_chunks):
                sc_copy(t, c, flipped(me, t, n)).wait_recv()

        for b in range(count):
            for c in range(col_chunks):
                wide = r_cols[owner_ref[first + b], c].astype(jnp.float32)
                out_ref[b, :, c * col_width : (c + 1) * col_width] = (
                    wide * ratios[b]
                ).astype(jnp.bfloat16)

        @pl.loop(1, n)
        def _(t):
            for c in range(col_chunks):
                sc_copy(t, c, me).wait_send()

        for s in range(row_chunks):
            z_rows(s).wait_send()

    @pl.loop(1, n)
    def _(t):
        g_copy(t, me).wait_send()
        a_copy(t, me).wait_send()
        q_copy(t, me).wait_send()


def on_device(grads, second_moment, root_factors, block_shape, block_owner):
    count, band, width = grads.shape
    n = lax.axis_size("fsdp")
    step_rows = max(band, 128)
    col_chunks = 8 if n <= 8 else 2
    row_chunks = width // step_rows
    col_width = width // col_chunks
    bf16, f32 = jnp.bfloat16, jnp.float32
    dma = pltpu.SemaphoreType.DMA
    return pl.pallas_call(
        functools.partial(kernel, n, step_rows, col_chunks),
        out_shape=jax.ShapeDtypeStruct(grads.shape, bf16),
        in_specs=[pl.BlockSpec(memory_space=pltpu.HBM)] * 5,
        out_specs=pl.BlockSpec(memory_space=pltpu.VMEM),
        scratch_shapes=[
            pltpu.SMEM((2, block_shape.shape[0]), jnp.int32),
            pltpu.SMEM(block_owner.shape, jnp.int32),
            pltpu.VMEM(grads.shape, bf16),
            pltpu.VMEM(grads.shape, bf16),
            dma((4,)),
            pltpu.VMEM((n, band, width), bf16),
            pltpu.VMEM((width, width), bf16),
            pltpu.VMEM((width, width), bf16),
            pltpu.VMEM((width, width), bf16),
            pltpu.VMEM((col_chunks, width, col_width), bf16),
            pltpu.VMEM((width, width), bf16),
            pltpu.VMEM((width, width), bf16),
            pltpu.VMEM((col_chunks, width, col_width), bf16),
            pltpu.VMEM((n, band, width), bf16),
            pltpu.VMEM((n, col_chunks, band, col_width), bf16),
            pltpu.VMEM((count, 8, 128), f32),
            pltpu.VMEM((n, count, 8, 128), f32),
            pltpu.VMEM((8, 128), f32),
            pltpu.VMEM((n, 8, 128), f32),
            dma,
            dma((n,)), dma((n,)), dma((n,)), dma((n,)), dma((n,)), dma((n,)),
            dma((row_chunks,)), dma((row_chunks,)),
            dma((col_chunks,)), dma((col_chunks,)),
            dma((n,)), dma((n,)),
            dma((n, col_chunks)), dma((n, col_chunks)),
        ],
        compiler_params=pltpu.CompilerParams(
            collective_id=0, has_side_effects=True, vmem_limit_bytes=60 * 1024 * 1024
        ),
        cost_estimate=pl.CostEstimate(
            flops=4 * width**3, bytes_accessed=4 * 1024 * 1024, transcendentals=0
        ),
    )(block_shape.T, block_owner, grads, second_moment, root_factors)


def solution(mesh):
    placed = (
        P("rep", "fsdp", None),
        P("rep", "fsdp", None),
        P("rep", "fsdp", None, None),
        P(),
        P(),
    )
    return jax.shard_map(
        on_device, mesh=mesh, in_specs=placed, out_specs=P("rep", "fsdp", None), check_vma=False
    )
```

```python
import functools

import jax
import jax.numpy as jnp
from jax import lax
from jax.experimental import pallas as pl
from jax.experimental.pallas import tpu as pltpu
from jax.sharding import PartitionSpec as P

ADAM_EPS = 1e-08
NORM_EPS = 1e-06
MESH = pl.DeviceIdType.MESH


def flipped(index, mask, extent):
    out, bit = 0, 1
    while bit < extent:
        out = out + bit * (((index // bit) % 2 + (mask // bit) % 2) % 2)
        bit *= 2
    return out


def fold(square):
    rows, columns = square.shape
    tall = jnp.sum(square.reshape(rows // 8, 8, columns), axis=0)
    return functools.reduce(
        lambda a, b: a + b, [tall[:, i : i + 128] for i in range(0, columns, 128)]
    )


def kernel(
    n, step_rows, col_chunks,
    shape_hbm, owner_hbm, grads_hbm, moment_hbm, factor_ref, out_ref,
    shape_ref, owner_ref, grads_ref, moment_ref, load_sem,
    outbound, g_full, own, other_rows, other_cols, half, s_rows, s_cols,
    r_rows, r_cols, adam_out, adam_in, sq_out, sq_in,
    own_sem, g_send, g_recv, a_send, a_recv, q_send, q_recv,
    zr_send, zr_recv, zc_send, zc_recv, sr_send, sr_recv, sc_send, sc_recv,
):
    count, band, width = grads_ref.shape
    me = lax.axis_index("fsdp")
    rep = lax.axis_index("rep")
    parity = rep % 2
    partner = rep + 1 - 2 * parity
    col_width = width // col_chunks
    row_chunks = width // step_rows
    group = step_rows // band
    near = n // 2
    first = rep * count

    barrier = pltpu.get_barrier_semaphore()

    @pl.loop(1, n)
    def _(t):
        pl.semaphore_signal(
            barrier, inc=1, device_id=(flipped(me, t, n), rep), device_id_type=MESH
        )

    pl.semaphore_signal(barrier, inc=1, device_id=(me, partner), device_id_type=MESH)

    loads = [
        pltpu.make_async_copy(source, target, load_sem.at[i])
        for i, (source, target) in enumerate([
            (shape_hbm, shape_ref), (owner_hbm, owner_ref),
            (grads_hbm, grads_ref), (moment_hbm, moment_ref),
        ])
    ]
    for load in loads:
        load.start()
    own_copy = pltpu.make_async_copy(factor_ref.at[0, 0], own, own_sem)
    own_copy.start()

    def rows_of(index):
        return pl.ds(pl.multiple_of(index * band, band), band)

    for load in loads[:3]:
        load.wait()

    line = me * band + lax.broadcasted_iota(jnp.int32, (band, width), 0)
    column = lax.broadcasted_iota(jnp.int32, (band, width), 1)
    masked = []
    for b in range(count):
        inside = (line < shape_ref[0, first + b]) & (column < shape_ref[1, first + b])
        wide = jnp.where(inside, grads_ref[b].astype(jnp.float32), 0.0)
        out_ref[b] = wide.astype(jnp.bfloat16)

    def fill(d):
        slot = jnp.zeros((band, width), jnp.bfloat16)
        for b in range(count):
            slot = jnp.where(owner_ref[first + b] == d, out_ref[b], slot)
        return slot

    @pl.loop(0, n)
    def _(d):
        outbound[d] = fill(d)

    g_full[rows_of(me)] = outbound[me]

    pl.semaphore_wait(barrier, n)

    def turn(s):
        if row_chunks != 8:
            return row_chunks - 1 - s
        late = s // 6
        return (1 - late) * (7 - 2 * (s % 3) - s // 3) + late * (7 - s)

    def z_rows(s):
        chunk = flipped(me // group, turn(s), row_chunks)
        rows = pl.ds(pl.multiple_of(chunk * step_rows, step_rows), step_rows)
        return pltpu.make_async_remote_copy(
            src_ref=factor_ref.at[0, 0, rows], dst_ref=other_rows.at[rows],
            send_sem=zr_send.at[s], recv_sem=zr_recv.at[s],
            device_id=(me, partner), device_id_type=MESH,
        )

    def z_cols(c):
        columns = pl.ds(c * col_width, col_width)
        return pltpu.make_async_remote_copy(
            src_ref=factor_ref.at[0, 0, :, columns], dst_ref=other_cols.at[c],
            send_sem=zc_send.at[c], recv_sem=zc_recv.at[c],
            device_id=(me, partner), device_id_type=MESH,
        )

    @pl.when(parity == 1)
    def _():
        for s in range(row_chunks):
            z_rows(s).start()

    @pl.when(parity == 0)
    def _():
        for c in range(col_chunks):
            z_cols(c).start()

    def peer_copy(source, target, send, recv, peer):
        return pltpu.make_async_remote_copy(
            src_ref=source, dst_ref=target, send_sem=send, recv_sem=recv,
            device_id=(peer, rep), device_id_type=MESH,
        )

    def g_copy(t, landing):
        peer = flipped(me, t, n)
        return peer_copy(
            outbound.at[peer], g_full.at[rows_of(landing)], g_send.at[t], g_recv.at[t], peer
        )

    @pl.loop(1, n)
    def _(s):
        g_copy(n - s, me).start()

    loads[3].wait()

    for b in range(count):
        adam = out_ref[b].astype(jnp.float32) / (
            jnp.sqrt(moment_ref[b].astype(jnp.float32)) + ADAM_EPS
        )
        adam_out[b] = fold(adam * adam)
    adam_in[me] = adam_out[...]

    def a_copy(t, landing):
        peer = flipped(me, t, n)
        return peer_copy(adam_out, adam_in.at[landing], a_send.at[t], a_recv.at[t], peer)

    def q_copy(t, landing):
        peer = flipped(me, t, n)
        return peer_copy(sq_out, sq_in.at[landing], q_send.at[t], q_recv.at[t], peer)

    @pl.loop(1, n)
    def _(t):
        a_copy(t, me).start()

    team_rows = jnp.int32(0)
    team_cols = jnp.int32(0)
    for b in range(count):
        mine = owner_ref[first + b] == me
        team_rows += jnp.where(mine, shape_ref[0, first + b], 0)
        team_cols += jnp.where(mine, shape_ref[1, first + b], 0)

    def clipped(full, row0, col0):
        r = row0 + lax.broadcasted_iota(jnp.int32, full.shape, 0)
        c = col0 + lax.broadcasted_iota(jnp.int32, full.shape, 1)
        return jnp.where((r < team_rows) & (c < team_cols), full, 0.0).astype(jnp.bfloat16)

    own_copy.wait()

    def sr_copy(t, landing):
        peer = flipped(me, t, n)
        return peer_copy(
            s_rows.at[rows_of(peer)], r_rows.at[landing], sr_send.at[t], sr_recv.at[t], peer
        )

    def sc_copy(t, c, landing):
        peer = flipped(me, t, n)
        return peer_copy(
            s_cols.at[c, rows_of(peer)], r_cols.at[landing, c],
            sc_send.at[t, c], sc_recv.at[t, c], peer,
        )

    @pl.when(parity == 0)
    def _():
        @pl.loop(0, n)
        def _(t):
            source = flipped(me, t, n)

            @pl.when(t != 0)
            def _():
                g_copy(t, source).wait_recv()

            half[rows_of(source)] = jnp.dot(
                g_full[rows_of(source)], own[...], preferred_element_type=jnp.float32
            ).astype(jnp.bfloat16)

        sq_out[...] = jnp.zeros_like(sq_out)

        @pl.loop(0, row_chunks)
        def _(s):
            z_rows(s).wait_recv()
            chunk = flipped(me // group, turn(s), row_chunks)
            row0 = pl.multiple_of(chunk * step_rows, step_rows)
            full = jnp.dot(
                other_rows[pl.ds(row0, step_rows)], half[...],
                preferred_element_type=jnp.float32,
            )
            part = clipped(full, row0, 0)
            s_rows[pl.ds(row0, step_rows)] = part
            for i in range(group):
                t = turn(s) * group + i

                @pl.when(t != 0)
                def _():
                    sr_copy(t, me).start()

            wide = part.astype(jnp.float32)
            sq_out[...] += fold(wide * wide)

        r_rows[me] = s_rows[rows_of(me)]

    @pl.when(parity == 1)
    def _():
        @pl.loop(1, n)
        def _(t):
            g_copy(t, flipped(me, t, n)).wait_recv()

        sq_out[...] = jnp.zeros_like(sq_out)

        @pl.loop(0, col_chunks)
        def _(c):
            pltpu.make_async_remote_copy(
                src_ref=other_cols.at[c], dst_ref=other_cols.at[c],
                send_sem=zc_send.at[c], recv_sem=zc_recv.at[c],
                device_id=(me, partner), device_id_type=MESH,
            ).wait_recv()
            h = jnp.dot(
                g_full[...], other_cols[c], preferred_element_type=jnp.float32
            ).astype(jnp.bfloat16)
            for far in (1, 0):
                side = flipped(me // near, far, 2)
                row0 = pl.multiple_of(side * (width // 2), width // 2)
                rows = pl.ds(row0, width // 2)
                full = jnp.dot(own[rows], h, preferred_element_type=jnp.float32)
                part = clipped(full, row0, c * col_width)
                s_cols[c, rows] = part

                @pl.loop(1 - far, near)
                def _(s):
                    sc_copy((1 + far) * near - 1 - s + (1 - far), c, me).start()

                wide = part.astype(jnp.float32)
                sq_out[...] += fold(wide * wide)

            r_cols[me, c] = s_cols[c, rows_of(me)]

    @pl.loop(1, n)
    def _(t):
        q_copy(t, me).start()

    sq_in[me] = sq_out[...]

    @pl.loop(1, n)
    def _(t):
        a_copy(t, flipped(me, t, n)).wait_recv()

    adam_sum = jnp.sum(adam_in[...], axis=0)

    @pl.loop(1, n)
    def _(t):
        q_copy(t, flipped(me, t, n)).wait_recv()

    ratios = []
    for b in range(count):
        adam_sq = jnp.sum(adam_sum[b], keepdims=True)
        shampoo_sq = jnp.sum(sq_in[owner_ref[first + b]], keepdims=True)
        ratios.append(jnp.sqrt(adam_sq) / jnp.sqrt(shampoo_sq + NORM_EPS))

    @pl.when(parity == 0)
    def _():
        @pl.loop(1, n)
        def _(t):
            sr_copy(t, flipped(me, t, n)).wait_recv()

        for b in range(count):
            wide = r_rows[owner_ref[first + b]].astype(jnp.float32)
            out_ref[b] = (wide * ratios[b]).astype(jnp.bfloat16)

        @pl.loop(1, n)
        def _(t):
            sr_copy(t, me).wait_send()

        for c in range(col_chunks):
            z_cols(c).wait_send()

    @pl.when(parity == 1)
    def _():
        @pl.loop(1, n)
        def _(t):
            for c in range(col_chunks):
                sc_copy(t, c, flipped(me, t, n)).wait_recv()

        for b in range(count):
            for c in range(col_chunks):
                wide = r_cols[owner_ref[first + b], c].astype(jnp.float32)
                out_ref[b, :, c * col_width : (c + 1) * col_width] = (
                    wide * ratios[b]
                ).astype(jnp.bfloat16)

        @pl.loop(1, n)
        def _(t):
            for c in range(col_chunks):
                sc_copy(t, c, me).wait_send()

        for s in range(row_chunks):
            z_rows(s).wait_send()

    @pl.loop(1, n)
    def _(t):
        g_copy(t, me).wait_send()
        a_copy(t, me).wait_send()
        q_copy(t, me).wait_send()


def on_device(grads, second_moment, root_factors, block_shape, block_owner):
    count, band, width = grads.shape
    n = lax.axis_size("fsdp")
    step_rows = max(band, 128)
    col_chunks = 8 if n <= 8 else 2
    row_chunks = width // step_rows
    col_width = width // col_chunks
    bf16, f32 = jnp.bfloat16, jnp.float32
    dma = pltpu.SemaphoreType.DMA
    return pl.pallas_call(
        functools.partial(kernel, n, step_rows, col_chunks),
        out_shape=jax.ShapeDtypeStruct(grads.shape, bf16),
        in_specs=[pl.BlockSpec(memory_space=pltpu.HBM)] * 5,
        out_specs=pl.BlockSpec(memory_space=pltpu.VMEM),
        scratch_shapes=[
            pltpu.SMEM((2, block_shape.shape[0]), jnp.int32),
            pltpu.SMEM(block_owner.shape, jnp.int32),
            pltpu.VMEM(grads.shape, bf16),
            pltpu.VMEM(grads.shape, bf16),
            dma((4,)),
            pltpu.VMEM((n, band, width), bf16),
            pltpu.VMEM((width, width), bf16),
            pltpu.VMEM((width, width), bf16),
            pltpu.VMEM((width, width), bf16),
            pltpu.VMEM((col_chunks, width, col_width), bf16),
            pltpu.VMEM((width, width), bf16),
            pltpu.VMEM((width, width), bf16),
            pltpu.VMEM((col_chunks, width, col_width), bf16),
            pltpu.VMEM((n, band, width), bf16),
            pltpu.VMEM((n, col_chunks, band, col_width), bf16),
            pltpu.VMEM((count, 8, 128), f32),
            pltpu.VMEM((n, count, 8, 128), f32),
            pltpu.VMEM((8, 128), f32),
            pltpu.VMEM((n, 8, 128), f32),
            dma,
            dma((n,)), dma((n,)), dma((n,)), dma((n,)), dma((n,)), dma((n,)),
            dma((row_chunks,)), dma((row_chunks,)),
            dma((col_chunks,)), dma((col_chunks,)),
            dma((n,)), dma((n,)),
            dma((n, col_chunks)), dma((n, col_chunks)),
        ],
        compiler_params=pltpu.CompilerParams(
            collective_id=0, has_side_effects=True, vmem_limit_bytes=60 * 1024 * 1024
        ),
        cost_estimate=pl.CostEstimate(
            flops=4 * width**3, bytes_accessed=4 * 1024 * 1024, transcendentals=0
        ),
    )(block_shape.T, block_owner, grads, second_moment, root_factors)


def solution(mesh):
    placed = (
        P("rep", "fsdp", None),
        P("rep", "fsdp", None),
        P("rep", "fsdp", None, None),
        P(),
        P(),
    )
    return jax.shard_map(
        on_device, mesh=mesh, in_specs=placed, out_specs=P("rep", "fsdp", None), check_vma=False
    )
```

```python
import functools

import jax
import jax.numpy as jnp
from jax import lax
from jax.experimental import pallas as pl
from jax.experimental.pallas import tpu as pltpu
from jax.sharding import PartitionSpec as P

ADAM_EPS = 1e-08
NORM_EPS = 1e-06
MESH = pl.DeviceIdType.MESH


def flipped(index, mask, extent):
    out, bit = 0, 1
    while bit < extent:
        out = out + bit * (((index // bit) % 2 + (mask // bit) % 2) % 2)
        bit *= 2
    return out


def fold(square):
    rows, columns = square.shape
    tall = jnp.sum(square.reshape(rows // 8, 8, columns), axis=0)
    return functools.reduce(
        lambda a, b: a + b, [tall[:, i : i + 128] for i in range(0, columns, 128)]
    )


def kernel(
    n, step_rows, col_chunks,
    shape_hbm, owner_hbm, grads_hbm, moment_hbm, factor_ref, out_ref,
    shape_ref, owner_ref, grads_ref, moment_ref, load_sem,
    outbound, g_full, own, other_rows, other_cols, half, s_rows, s_cols,
    r_rows, r_cols, adam_out, adam_in, sq_out, sq_in,
    own_sem, g_send, g_recv, a_send, a_recv, q_send, q_recv,
    zr_send, zr_recv, zc_send, zc_recv, sr_send, sr_recv, sc_send, sc_recv,
):
    count, band, width = grads_ref.shape
    me = lax.axis_index("fsdp")
    rep = lax.axis_index("rep")
    parity = rep % 2
    partner = rep + 1 - 2 * parity
    col_width = width // col_chunks
    row_chunks = width // step_rows
    group = step_rows // band
    near = n // 2
    first = rep * count

    barrier = pltpu.get_barrier_semaphore()

    @pl.loop(1, n)
    def _(t):
        pl.semaphore_signal(
            barrier, inc=1, device_id=(flipped(me, t, n), rep), device_id_type=MESH
        )

    pl.semaphore_signal(barrier, inc=1, device_id=(me, partner), device_id_type=MESH)

    loads = [
        pltpu.make_async_copy(source, target, load_sem.at[i])
        for i, (source, target) in enumerate([
            (shape_hbm, shape_ref), (owner_hbm, owner_ref),
            (grads_hbm, grads_ref), (moment_hbm, moment_ref),
        ])
    ]
    for load in loads:
        load.start()
    own_copy = pltpu.make_async_copy(factor_ref.at[0, 0], own, own_sem)
    own_copy.start()

    def rows_of(index):
        return pl.ds(pl.multiple_of(index * band, band), band)

    for load in loads[:3]:
        load.wait()

    line = me * band + lax.broadcasted_iota(jnp.int32, (band, width), 0)
    column = lax.broadcasted_iota(jnp.int32, (band, width), 1)
    masked = []
    for b in range(count):
        inside = (line < shape_ref[0, first + b]) & (column < shape_ref[1, first + b])
        wide = jnp.where(inside, grads_ref[b].astype(jnp.float32), 0.0)
        out_ref[b] = wide.astype(jnp.bfloat16)

    def fill(d):
        slot = jnp.zeros((band, width), jnp.bfloat16)
        for b in range(count):
            slot = jnp.where(owner_ref[first + b] == d, out_ref[b], slot)
        return slot

    @pl.loop(0, n)
    def _(d):
        outbound[d] = fill(d)

    g_full[rows_of(me)] = outbound[me]

    pl.semaphore_wait(barrier, n)

    def turn(s):
        if row_chunks != 8:
            return row_chunks - 1 - s
        late = s // 6
        return (1 - late) * (7 - 2 * (s % 3) - s // 3) + late * (7 - s)

    def z_rows(s):
        chunk = flipped(me // group, turn(s), row_chunks)
        rows = pl.ds(pl.multiple_of(chunk * step_rows, step_rows), step_rows)
        return pltpu.make_async_remote_copy(
            src_ref=factor_ref.at[0, 0, rows], dst_ref=other_rows.at[rows],
            send_sem=zr_send.at[s], recv_sem=zr_recv.at[s],
            device_id=(me, partner), device_id_type=MESH,
        )

    def z_cols(c):
        columns = pl.ds(c * col_width, col_width)
        return pltpu.make_async_remote_copy(
            src_ref=factor_ref.at[0, 0, :, columns], dst_ref=other_cols.at[c],
            send_sem=zc_send.at[c], recv_sem=zc_recv.at[c],
            device_id=(me, partner), device_id_type=MESH,
        )

    @pl.when(parity == 1)
    def _():
        for s in range(row_chunks):
            z_rows(s).start()

    @pl.when(parity == 0)
    def _():
        for c in range(col_chunks):
            z_cols(c).start()

    def peer_copy(source, target, send, recv, peer):
        return pltpu.make_async_remote_copy(
            src_ref=source, dst_ref=target, send_sem=send, recv_sem=recv,
            device_id=(peer, rep), device_id_type=MESH,
        )

    def g_copy(t, landing):
        peer = flipped(me, t, n)
        return peer_copy(
            outbound.at[peer], g_full.at[rows_of(landing)], g_send.at[t], g_recv.at[t], peer
        )

    @pl.loop(1, n)
    def _(s):
        g_copy(n - s, me).start()

    loads[3].wait()

    for b in range(count):
        adam = out_ref[b].astype(jnp.float32) / (
            jnp.sqrt(moment_ref[b].astype(jnp.float32)) + ADAM_EPS
        )
        adam_out[b] = fold(adam * adam)
    adam_in[me] = adam_out[...]

    def a_copy(t, landing):
        peer = flipped(me, t, n)
        return peer_copy(adam_out, adam_in.at[landing], a_send.at[t], a_recv.at[t], peer)

    def q_copy(t, landing):
        peer = flipped(me, t, n)
        return peer_copy(sq_out, sq_in.at[landing], q_send.at[t], q_recv.at[t], peer)

    @pl.loop(1, n)
    def _(t):
        a_copy(t, me).start()

    team_rows = jnp.int32(0)
    team_cols = jnp.int32(0)
    for b in range(count):
        mine = owner_ref[first + b] == me
        team_rows += jnp.where(mine, shape_ref[0, first + b], 0)
        team_cols += jnp.where(mine, shape_ref[1, first + b], 0)

    def clipped(full, row0, col0):
        r = row0 + lax.broadcasted_iota(jnp.int32, full.shape, 0)
        c = col0 + lax.broadcasted_iota(jnp.int32, full.shape, 1)
        return jnp.where((r < team_rows) & (c < team_cols), full, 0.0).astype(jnp.bfloat16)

    own_copy.wait()

    def sr_copy(t, landing):
        peer = flipped(me, t, n)
        return peer_copy(
            s_rows.at[rows_of(peer)], r_rows.at[landing], sr_send.at[t], sr_recv.at[t], peer
        )

    def sc_copy(t, c, landing):
        peer = flipped(me, t, n)
        return peer_copy(
            s_cols.at[c, rows_of(peer)], r_cols.at[landing, c],
            sc_send.at[t, c], sc_recv.at[t, c], peer,
        )

    @pl.when(parity == 0)
    def _():
        @pl.loop(0, n)
        def _(t):
            source = flipped(me, t, n)

            @pl.when(t != 0)
            def _():
                g_copy(t, source).wait_recv()

            half[rows_of(source)] = jnp.dot(
                g_full[rows_of(source)], own[...], preferred_element_type=jnp.float32
            ).astype(jnp.bfloat16)

        sq_out[...] = jnp.zeros_like(sq_out)

        @pl.loop(0, row_chunks)
        def _(s):
            z_rows(s).wait_recv()
            chunk = flipped(me // group, turn(s), row_chunks)
            row0 = pl.multiple_of(chunk * step_rows, step_rows)
            full = jnp.dot(
                other_rows[pl.ds(row0, step_rows)], half[...],
                preferred_element_type=jnp.float32,
            )
            part = clipped(full, row0, 0)
            s_rows[pl.ds(row0, step_rows)] = part
            for i in range(group):
                t = turn(s) * group + i

                @pl.when(t != 0)
                def _():
                    sr_copy(t, me).start()

            wide = part.astype(jnp.float32)
            sq_out[...] += fold(wide * wide)

        r_rows[me] = s_rows[rows_of(me)]

    @pl.when(parity == 1)
    def _():
        def z_arrived(c):
            pltpu.make_async_remote_copy(
                src_ref=other_cols.at[c], dst_ref=other_cols.at[c],
                send_sem=zc_send.at[c], recv_sem=zc_recv.at[c],
                device_id=(me, partner), device_id_type=MESH,
            ).wait_recv()

        z_arrived(0)

        @pl.loop(0, n)
        def _(t):
            source = flipped(me, t, n)

            @pl.when(t != 0)
            def _():
                g_copy(t, source).wait_recv()

            half[rows_of(source), 0:col_width] = jnp.dot(
                g_full[rows_of(source)], other_cols[0], preferred_element_type=jnp.float32
            ).astype(jnp.bfloat16)

        sq_out[...] = jnp.zeros_like(sq_out)

        @pl.loop(0, col_chunks)
        def _(c):
            @pl.when(c != 0)
            def _():
                z_arrived(c)
                half[:, 0:col_width] = jnp.dot(
                    g_full[...], other_cols[c], preferred_element_type=jnp.float32
                ).astype(jnp.bfloat16)

            h = half[:, 0:col_width]
            for far in (1, 0):
                side = flipped(me // near, far, 2)
                row0 = pl.multiple_of(side * (width // 2), width // 2)
                rows = pl.ds(row0, width // 2)
                full = jnp.dot(own[rows], h, preferred_element_type=jnp.float32)
                part = clipped(full, row0, c * col_width)
                s_cols[c, rows] = part

                @pl.loop(1 - far, near)
                def _(s):
                    sc_copy((1 + far) * near - 1 - s + (1 - far), c, me).start()

                wide = part.astype(jnp.float32)
                sq_out[...] += fold(wide * wide)

            r_cols[me, c] = s_cols[c, rows_of(me)]

    @pl.loop(1, n)
    def _(t):
        q_copy(t, me).start()

    sq_in[me] = sq_out[...]

    @pl.loop(1, n)
    def _(t):
        a_copy(t, flipped(me, t, n)).wait_recv()

    adam_sum = jnp.sum(adam_in[...], axis=0)

    @pl.loop(1, n)
    def _(t):
        q_copy(t, flipped(me, t, n)).wait_recv()

    ratios = []
    for b in range(count):
        adam_sq = jnp.sum(adam_sum[b], keepdims=True)
        shampoo_sq = jnp.sum(sq_in[owner_ref[first + b]], keepdims=True)
        ratios.append(jnp.sqrt(adam_sq) / jnp.sqrt(shampoo_sq + NORM_EPS))

    @pl.when(parity == 0)
    def _():
        @pl.loop(1, n)
        def _(t):
            sr_copy(t, flipped(me, t, n)).wait_recv()

        for b in range(count):
            wide = r_rows[owner_ref[first + b]].astype(jnp.float32)
            out_ref[b] = (wide * ratios[b]).astype(jnp.bfloat16)

        @pl.loop(1, n)
        def _(t):
            sr_copy(t, me).wait_send()

        for c in range(col_chunks):
            z_cols(c).wait_send()

    @pl.when(parity == 1)
    def _():
        @pl.loop(1, n)
        def _(t):
            for c in range(col_chunks):
                sc_copy(t, c, flipped(me, t, n)).wait_recv()

        for b in range(count):
            for c in range(col_chunks):
                wide = r_cols[owner_ref[first + b], c].astype(jnp.float32)
                out_ref[b, :, c * col_width : (c + 1) * col_width] = (
                    wide * ratios[b]
                ).astype(jnp.bfloat16)

        @pl.loop(1, n)
        def _(t):
            for c in range(col_chunks):
                sc_copy(t, c, me).wait_send()

        for s in range(row_chunks):
            z_rows(s).wait_send()

    @pl.loop(1, n)
    def _(t):
        g_copy(t, me).wait_send()
        a_copy(t, me).wait_send()
        q_copy(t, me).wait_send()


def on_device(grads, second_moment, root_factors, block_shape, block_owner):
    count, band, width = grads.shape
    n = lax.axis_size("fsdp")
    step_rows = max(band, 128)
    col_chunks = 8 if n <= 8 else 2
    row_chunks = width // step_rows
    col_width = width // col_chunks
    bf16, f32 = jnp.bfloat16, jnp.float32
    dma = pltpu.SemaphoreType.DMA
    return pl.pallas_call(
        functools.partial(kernel, n, step_rows, col_chunks),
        out_shape=jax.ShapeDtypeStruct(grads.shape, bf16),
        in_specs=[pl.BlockSpec(memory_space=pltpu.HBM)] * 5,
        out_specs=pl.BlockSpec(memory_space=pltpu.VMEM),
        scratch_shapes=[
            pltpu.SMEM((2, block_shape.shape[0]), jnp.int32),
            pltpu.SMEM(block_owner.shape, jnp.int32),
            pltpu.VMEM(grads.shape, bf16),
            pltpu.VMEM(grads.shape, bf16),
            dma((4,)),
            pltpu.VMEM((n, band, width), bf16),
            pltpu.VMEM((width, width), bf16),
            pltpu.VMEM((width, width), bf16),
            pltpu.VMEM((width, width), bf16),
            pltpu.VMEM((col_chunks, width, col_width), bf16),
            pltpu.VMEM((width, width), bf16),
            pltpu.VMEM((width, width), bf16),
            pltpu.VMEM((col_chunks, width, col_width), bf16),
            pltpu.VMEM((n, band, width), bf16),
            pltpu.VMEM((n, col_chunks, band, col_width), bf16),
            pltpu.VMEM((count, 8, 128), f32),
            pltpu.VMEM((n, count, 8, 128), f32),
            pltpu.VMEM((8, 128), f32),
            pltpu.VMEM((n, 8, 128), f32),
            dma,
            dma((n,)), dma((n,)), dma((n,)), dma((n,)), dma((n,)), dma((n,)),
            dma((row_chunks,)), dma((row_chunks,)),
            dma((col_chunks,)), dma((col_chunks,)),
            dma((n,)), dma((n,)),
            dma((n, col_chunks)), dma((n, col_chunks)),
        ],
        compiler_params=pltpu.CompilerParams(
            collective_id=0, has_side_effects=True, vmem_limit_bytes=60 * 1024 * 1024
        ),
        cost_estimate=pl.CostEstimate(
            flops=4 * width**3, bytes_accessed=4 * 1024 * 1024, transcendentals=0
        ),
    )(block_shape.T, block_owner, grads, second_moment, root_factors)


def solution(mesh):
    placed = (
        P("rep", "fsdp", None),
        P("rep", "fsdp", None),
        P("rep", "fsdp", None, None),
        P(),
        P(),
    )
    return jax.shard_map(
        on_device, mesh=mesh, in_specs=placed, out_specs=P("rep", "fsdp", None), check_vma=False
    )
```
